32 devices in a mesh: groups: 2 (over x), ctx: 16 (over z, y, core).
Axes of the slice: x: 2, y: 2, z: 4, core: 2. Of those that a mesh axis runs over, the one named last changes fastest.
Arguments:
- hidden: bfloat16 [24576, 4096], P(('groups', 'ctx')), parts along dimension 0, may hold values from -6 to 6
- w_qkv: bfloat16 [4096, 768], P('ctx'), may hold values from -0.09375 to 0.09375
- w_out: bfloat16 [256, 4096], P('ctx'), may hold values from -0.375 to 0.375
- norm_gain: float32 [256], replicated, may hold values from 0.1 to 1.9
- incoming: float32 [4, 128, 128], P('groups'), parts along dimension 0, may hold values from -600 to 600
Outputs:
- attn_out: bfloat16 [24576, 4096], P(('groups', 'ctx')), parts along dimension 0
The draws below stay inside these ranges and needn't reach their ends.
There are 2 independent parts, one for each index of `groups`. The reference program is written for one: setup_inputs(seed, part) draws one part's arguments, and reference() takes and returns one part's arrays. A program takes and returns all parts, laid end to end along the dimension named above; an argument that names none is the same for every part. Nothing has to cross between parts.
All inputs are finite; a program needn't handle non-finite values.
Results may differ from the reference program's by a relative error of at most 0.0065.
Values may be sent and summed in bfloat16 or wider, within the bound.
A program may use at most 64 MiB of HBM per device.

```python
import jax
import jax.numpy as jnp
from jax import lax

D = 4096
HEAD_DIM = 128
HEADS = 2
TOK_DEV = 768
HD = 256
TOKENS = 12288
N_CTX = 16


def levels(stream_key, shape, shards, low, top_value):
    def one(dim, blocks):
        heights = jax.random.uniform(jax.random.fold_in(jax.random.fold_in(stream_key, 6), dim), (blocks,), jnp.float32, low / len(shards), top_value / len(shards))
        return jnp.repeat(jnp.exp(heights), shape[dim] // blocks).reshape((-1,) + (1,) * (len(shape) - dim - 1))

    factor_of = one(*shards[0])
    for cut in shards[1:]:
        factor_of = factor_of * one(*cut)
    return factor_of


def gaussian(stream_key, shape, scale, bound, split=(), held_as=jnp.bfloat16):
    values = jax.random.normal(stream_key, shape, jnp.float32) * scale
    if len(split) > 0:
        values = levels(stream_key, shape, split, -0.22, 0.18) * values
    return jnp.clip(values, min=-bound, max=bound).astype(held_as)


def setup_inputs(seed: int = 0, part: int = 0) -> dict:
    key_list = jax.random.split(jax.random.key(seed), 6)
    part_keys = jax.random.split(jax.random.fold_in(key_list[5], part), 6)
    hidden = gaussian(part_keys[0], (TOKENS, D), 1.0, 6.0, ((0, 16),))
    w_qkv = gaussian(key_list[1], (D, 3 * HD), D ** -0.5, 0.09375, ((0, 16),))
    w_out = gaussian(key_list[2], (HD, D), HD ** -0.5, 0.375, ((0, 16),))
    norm_gain = jnp.clip(1.0 + 0.18 * jax.random.normal(key_list[3], (HD,), jnp.float32), 0.1, 1.9)
    incoming = gaussian(part_keys[4], (HEADS, HEAD_DIM, HEAD_DIM), 100.0, 600.0, (), jnp.float32)
    return dict(hidden=hidden, w_qkv=w_qkv, w_out=w_out, norm_gain=norm_gain, incoming=incoming)


def reference(hidden, w_qkv, w_out, norm_gain, incoming):
    width = HEADS * HEAD_DIM
    proj = jnp.dot(hidden, w_qkv, preferred_element_type=jnp.float32).astype(jnp.bfloat16)
    parts = proj.reshape(N_CTX, TOK_DEV, 3, HEADS, HEAD_DIM).astype(jnp.float32)
    query = parts[:, :, 0]
    keys = parts[:, :, 1]
    values = parts[:, :, 2]
    states = jnp.einsum('bthd,bthe->bhde', keys, values, precision=lax.Precision.HIGHEST)
    before = jnp.concatenate([jnp.zeros((1, HEADS, HEAD_DIM, HEAD_DIM), jnp.float32), jnp.cumsum(states, axis=0)[:-1]], axis=0)
    prior = incoming[None] + before
    gains = norm_gain.reshape(HEADS, HEAD_DIM)
    rows = jnp.arange(TOK_DEV)
    causal = rows[:, None] >= rows[None, :]

    def one_block(items):
        qry, key_blk, val_blk, state = items
        scores = jnp.einsum('thd,shd->hts', qry, key_blk, precision=lax.Precision.HIGHEST)
        scores = jnp.where(causal[None], scores, 0.0).astype(jnp.bfloat16)
        scores = lax.optimization_barrier(scores).astype(jnp.float32)
        intra = jnp.einsum('hts,she->the', scores, val_blk, precision=lax.Precision.HIGHEST)
        cross = jnp.einsum('thd,hde->the', qry, state, precision=lax.Precision.HIGHEST)
        mixed = intra + cross
        scale = lax.rsqrt(lax.optimization_barrier(jnp.mean(mixed * mixed, axis=-1, keepdims=True)) + 1e-06)
        return (mixed * scale * gains).astype(jnp.bfloat16).reshape(TOK_DEV, width)
    normed = lax.map(one_block, (query, keys, values, prior)).reshape(N_CTX * TOK_DEV, width)
    return jnp.dot(normed, w_out, preferred_element_type=jnp.float32).astype(jnp.bfloat16)
```

```python
import functools

import jax
import jax.numpy as jnp
from jax import lax
from jax.experimental import pallas as pl
from jax.experimental.pallas import tpu as pltpu
from jax.sharding import PartitionSpec as P

MESH = pl.DeviceIdType.MESH
CORES = 2
RIGHT, LEFT = 0, 1


def bands(units, first):
    third = units * 5 // 16 if first else -(-units * 5 // 16)
    return third, units - 2 * third


def kernel(
    n_groups, n_ctx, heads, head_size, rows, o_cols,
    hid_hbm, wq_hbm, wo_hbm, gain_ref, inc_ref,
    normed_ref, wo_all,
    hid, wq, acc, proj, st_mine, st_peer, st_out, st_in, st_half, st_other,
    load_sem, ring_send, ring_recv, x_send, x_recv, sa_send, sa_recv, sb_send, sb_recv,
    own_send, own_recv, t_send, t_recv, p_send, p_recv,
):
    n = n_ctx // CORES
    half = n // 2
    snake = 2 if n == 8 else 1
    tokens = hid.shape[0]
    width = heads * head_size
    group = lax.axis_index("groups")
    ctx = lax.axis_index("ctx")
    core = lax.rem(ctx, CORES)
    chip = ctx // CORES
    side = lax.rem(group, 2)
    partner = (group + 1 - 2 * side, ctx)
    peer_ctx = ctx + 1 - 2 * core
    peer = (group, peer_ctx)

    def fold(k):
        if snake == 1:
            return k
        y = lax.rem(k, 2)
        z = k // 2
        return z + y * (n - 1 - 2 * z)

    def unfold(p):
        if snake == 1:
            return p
        y = p // (n // 2)
        z = p + y * (n - 1 - 2 * p)
        return z * 2 + y

    place = fold(chip)

    def chip_at(delta):
        return unfold(lax.rem(place + delta + 2 * n, n))

    to_right = (group, chip_at(1) * CORES + core)
    to_left = (group, chip_at(-1) * CORES + core)

    streams = []
    q_units = rows // 16 // 2
    o_units = o_cols // 128 // 2
    for u in range(2):
        b, a = bands(q_units, u == 0)
        streams.append((0, u * q_units * 16, b * 16, a * 16))
    for u in range(2):
        b, a = bands(o_units, u == 0)
        streams.append((1, u * o_units * 128, b * 128, a * 128))
    use_x = n_groups % 2 == 0
    if not use_x:
        streams = [(k, base, 0, 2 * b + a) for k, base, b, a in streams]
    hops = [(half, n - 1 - half), (n - 1 - half, half)] * 2

    def part(kind, dev, start, size):
        if kind == 0:
            at = pl.multiple_of(dev * rows + start, 16)
            return wq.at[pl.ds(at, size), :]
        return wo_all.at[dev, :, pl.ds(pl.multiple_of(start, 128), size)]

    def ring_part(s, dev):
        kind, base, b, a = streams[s]
        return part(kind, dev, base + side * b, a + b)

    def x_part(s, dev, mine):
        kind, base, b, a = streams[s]
        who = side if mine else 1 - side
        return part(kind, dev, base + who * (a + b), b)

    def whole_part(s, dev):
        kind, base, b, a = streams[s]
        return part(kind, dev, base, a + 2 * b)

    def source(d, h, c):
        return chip_at(-h if d == RIGHT else h) * CORES + c

    def remote(ref, send, recv, target, dst=None):
        return pltpu.make_async_remote_copy(
            src_ref=ref, dst_ref=ref if dst is None else dst, send_sem=send,
            recv_sem=recv, device_id=target, device_id_type=MESH,
        )

    def ring_copy(s, d, h):
        return remote(
            ring_part(s, source(d, h - 1, core)), ring_send.at[s, d, h], ring_recv.at[s, d, h],
            to_right if d == RIGHT else to_left,
        )

    def x_copy(s, d, h, mine=True):
        return remote(x_part(s, source(d, h, core), mine), x_send.at[s, d, h], x_recv.at[s, d, h], partner)

    def sib_ring(s, d, h, c):
        return remote(ring_part(s, source(d, h, c)), sa_send.at[s, d, h], sa_recv.at[s, d, h], peer)

    def sib_x(s, d, h, c):
        return remote(x_part(s, source(d, h, c), False), sb_send.at[s, d, h], sb_recv.at[s, d, h], peer)

    def sib_own(s, dev):
        return remote(whole_part(s, dev), own_send.at[s], own_recv.at[s], peer)

    loads = [
        pltpu.make_async_copy(wq_hbm, wq.at[pl.ds(pl.multiple_of(ctx * rows, 16), rows), :], load_sem.at[0]),
        pltpu.make_async_copy(wo_hbm, wo_all.at[ctx], load_sem.at[1]),
        pltpu.make_async_copy(hid_hbm, hid, load_sem.at[2]),
    ]
    for load in loads:
        load.start()

    barrier = pltpu.get_barrier_semaphore()
    for j in range(1, n):
        other = lax.rem(chip + j, n) * CORES + core
        pl.semaphore_signal(barrier, inc=1, device_id=(group, other), device_id_type=MESH)
    pl.semaphore_signal(barrier, inc=1, device_id=peer, device_id_type=MESH)
    if use_x:
        pl.semaphore_signal(barrier, inc=1, device_id=partner, device_id_type=MESH)
    pl.semaphore_wait(barrier, n + (1 if use_x else 0))

    sent = []

    def go(copy):
        copy.start()
        sent.append(copy)

    def start_stream(s):
        for d in (RIGHT, LEFT):
            if hops[s][d] >= 1:
                go(ring_copy(s, d, 1))
        go(sib_own(s, ctx))

    def arrive(s, d, h):
        ring_copy(s, d, h).wait_recv()
        if h + 1 <= hops[s][d]:
            go(ring_copy(s, d, h + 1))
        if use_x and streams[s][2]:
            go(x_copy(s, d, h))
        go(sib_ring(s, d, h, core))

    def arrive_x(s, d, h):
        if use_x and streams[s][2]:
            x_copy(s, d, h, False).wait_recv()
            go(sib_x(s, d, h, core))

    def settle(s, d, h):
        sib_ring(s, d, h, 1 - core).wait_recv()
        if use_x and streams[s][2]:
            sib_x(s, d, h, 1 - core).wait_recv()

    tile = 256 if tokens % 256 == 0 else tokens

    def accumulate(which, first=False):
        at = pl.multiple_of(which * (CORES * rows), 128)
        depth = pl.ds(at, CORES * rows)

        @pl.loop(0, tokens // tile)
        def _(i):
            r = pl.ds(pl.multiple_of(i * tile, tile), tile)
            term = jnp.dot(hid[r, depth], wq[depth, :], preferred_element_type=jnp.float32)
            if first:
                acc[r, :] = term
            else:
                acc[r, :] += term

    def items(pair):
        found = []
        for h in range(1, half + 1):
            for s in pair:
                for d in (RIGHT, LEFT):
                    if h <= hops[s][d]:
                        found.append((s, d, h))
        return found

    loads[0].wait()
    for s in (0, 1):
        start_stream(s)
    loads[1].wait()
    loads[2].wait()
    for s in (0, 1):
        sib_own(s, peer_ctx).wait_recv()
    accumulate(chip, first=True)

    def chip_key(s, d, h):
        return h if d == RIGHT else n - h

    pending = {}
    for s, d, h in items((0, 1)):
        pending.setdefault(chip_key(s, d, h), []).append((s, d, h))

    queue = items((0, 1))
    settled = {}
    lag_x, lag_sum = 2, 5
    length = len(queue)
    for i in range(length + lag_sum):
        if i < length:
            if i == length - 2:
                for s in (2, 3):
                    start_stream(s)
            arrive(*queue[i])
        if 0 <= i - lag_x < length:
            arrive_x(*queue[i - lag_x])
        if 0 <= i - lag_sum < length:
            item = queue[i - lag_sum]
            settle(*item)
            key = chip_key(*item)
            settled[key] = settled.get(key, 0) + 1
            if settled[key] == len(pending[key]):
                accumulate(chip_at(-key))

    o_queue = items((2, 3))
    o_lag = 2
    o_state = [0]

    def o_steps(count):
        for _ in range(count):
            i = o_state[0]
            if i < len(o_queue):
                arrive(*o_queue[i])
            if 0 <= i - o_lag < len(o_queue):
                arrive_x(*o_queue[i - o_lag])
            o_state[0] = i + 1

    o_steps(4)
    proj[...] = acc[...].astype(jnp.bfloat16)

    def cols(kind, h):
        at = kind * width + h * head_size
        return slice(at, at + head_size)

    for h in range(heads):
        st_mine[h] = lax.dot_general(
            proj[:, cols(1, h)], proj[:, cols(2, h)], (((0,), (0,)), ((), ())),
            preferred_element_type=jnp.float32,
        )
    state_copy = remote(st_mine, t_send.at[0], t_recv.at[0], peer, st_peer)
    go(state_copy)

    share = heads // CORES

    def intra(h):
        for i in range(tokens // tile):
            r = slice(i * tile, (i + 1) * tile)
            upto = slice(0, (i + 1) * tile)
            scores = lax.dot_general(
                proj[r, cols(0, h)], proj[upto, cols(1, h)], (((1,), (1,)), ((), ())),
                preferred_element_type=jnp.float32,
            )
            row = lax.broadcasted_iota(jnp.int32, scores.shape, 0) + i * tile
            col = lax.broadcasted_iota(jnp.int32, scores.shape, 1)
            scores = jnp.where(row >= col, scores, 0.0).astype(jnp.bfloat16)
            acc[r, h * head_size : (h + 1) * head_size] = jnp.dot(
                scores, proj[upto, cols(2, h)], preferred_element_type=jnp.float32
            )

    state_copy.wait_recv()
    mine = pl.ds(core * share, share)
    st_out[...] = (st_mine[mine] + st_peer[mine]).astype(st_out.dtype)

    def state_to(j):
        target = lax.rem(chip + j, n) * CORES + core
        return remote(st_out, p_send.at[j], p_recv.at[j], (group, target), st_in.at[j])

    for j in range(1, n):
        @pl.when(chip + j < n)
        def _():
            state_to(j).start()

    o_steps(2)
    intra(0)
    o_steps(2)
    for h in range(1, heads):
        intra(h)

    st_half[...] = jnp.zeros_like(st_half)
    for j in range(1, n):
        @pl.when(chip >= j)
        def _():
            state_to(j).wait_recv()
            st_half[...] += st_in[j].astype(jnp.float32)

    half_copy = remote(st_half, t_send.at[1], t_recv.at[1], peer, st_other)
    go(half_copy)
    o_steps(2)
    half_copy.wait_recv()

    after = core.astype(jnp.float32)
    for h in range(heads):
        own = (h // share) == core
        low = st_half[h % share]
        high = st_other[h % share]
        prior = inc_ref[h] + jnp.where(own, low, high) + after * st_peer[h]
        top = prior.astype(jnp.bfloat16)
        rest = (prior - top.astype(jnp.float32)).astype(jnp.bfloat16)
        o = slice(h * head_size, (h + 1) * head_size)
        for i in range(tokens // tile):
            r = slice(i * tile, (i + 1) * tile)
            query = proj[r, cols(0, h)]
            mixed = (
                acc[r, o]
                + jnp.dot(query, top, preferred_element_type=jnp.float32)
                + jnp.dot(query, rest, preferred_element_type=jnp.float32)
            )
            scale = lax.rsqrt(jnp.mean(mixed * mixed, axis=-1, keepdims=True) + 1e-06)
            normed_ref[r, o] = (mixed * scale * gain_ref[:, o]).astype(jnp.bfloat16)

    o_steps(len(o_queue) + o_lag - o_state[0])
    for s in (2, 3):
        sib_own(s, peer_ctx).wait_recv()
    for item in o_queue:
        settle(*item)
    for copy in sent:
        copy.wait_send()
    for j in range(1, n):
        @pl.when(chip + j < n)
        def _():
            state_to(j).wait_send()


def local(n_groups, n_ctx, hidden, w_qkv, w_out, norm_gain, incoming):
    tokens, model = hidden.shape
    rows, three = w_qkv.shape
    heads, head_size, _ = incoming.shape
    width = three // 3
    out_rows, out_cols = w_out.shape
    fine = w_out.reshape(16, out_rows * out_cols // 16)
    o_cols = fine.shape[1]
    n = n_ctx // CORES
    half = n // 2
    share = heads // CORES
    dma = pltpu.SemaphoreType.DMA
    state = (heads, head_size, head_size)
    part = (share, head_size, head_size)
    flops = 2 * tokens * model * three
    normed, w_all = pl.pallas_call(
        functools.partial(kernel, n_groups, n_ctx, heads, head_size, rows, o_cols),
        out_shape=(
            jax.ShapeDtypeStruct((tokens, width), jnp.bfloat16),
            jax.ShapeDtypeStruct((n_ctx, 16, o_cols), jnp.bfloat16),
        ),
        in_specs=[pl.BlockSpec(memory_space=pl.ANY)] * 3
        + [pl.BlockSpec(memory_space=pltpu.VMEM)] * 2,
        out_specs=(
            pl.BlockSpec(memory_space=pltpu.VMEM),
            pl.BlockSpec(memory_space=pl.ANY),
        ),
        scratch_shapes=[
            pltpu.VMEM((tokens, model), jnp.bfloat16),
            pltpu.VMEM((model, three), jnp.bfloat16),
            pltpu.VMEM((tokens, three), jnp.float32),
            pltpu.VMEM((tokens, three), jnp.bfloat16),
            pltpu.VMEM(state, jnp.float32),
            pltpu.VMEM(state, jnp.float32),
            pltpu.VMEM(part, jnp.bfloat16),
            pltpu.VMEM((n,) + part, jnp.bfloat16),
            pltpu.VMEM(part, jnp.float32),
            pltpu.VMEM(part, jnp.float32),
            dma((3,)),
        ]
        + [dma((4, 2, half + 1))] * 8
        + [dma((4,)), dma((4,)), dma((2,)), dma((2,)), dma((n,)), dma((n,))],
        compiler_params=pltpu.CompilerParams(
            collective_id=0, has_side_effects=True, vmem_limit_bytes=48 * 1024 * 1024
        ),
        cost_estimate=pl.CostEstimate(
            flops=flops, bytes_accessed=tokens * model * 2, transcendentals=0
        ),
    )(hidden, w_qkv, fine, norm_gain.reshape(1, width), incoming)
    w_full = w_all.reshape(n_ctx * out_rows, out_cols)
    result = jnp.dot(normed, w_full, preferred_element_type=jnp.float32)
    return result.astype(jnp.bfloat16)


def solution(mesh):
    body = functools.partial(local, mesh.shape["groups"], mesh.shape["ctx"])
    return jax.shard_map(
        body,
        mesh=mesh,
        in_specs=(
            P(("groups", "ctx"), None),
            P("ctx", None),
            P("ctx", None),
            P(),
            P("groups", None, None),
        ),
        out_specs=P(("groups", "ctx"), None),
        check_vma=False,
    )
```

```python
import functools

import jax
import jax.numpy as jnp
from jax import lax
from jax.experimental import pallas as pl
from jax.experimental.pallas import tpu as pltpu
from jax.sharding import PartitionSpec as P

MESH = pl.DeviceIdType.MESH
CORES = 2
RIGHT, LEFT = 0, 1
LAG_X, LAG_SUM = 12, 22


def shares(units, count):
    if units == 16 and count == 4:
        return [(1, 1), (1, 1), (2, 1), (1, 3)]
    sizes = [units * (i + 1) // count - units * i // count for i in range(count)]
    outer = [min((5 * size + (15 if i % 2 else 0)) // 16, size // 2) for i, size in enumerate(sizes)]
    return [(b, size - 2 * b) for b, size in zip(outer, sizes)]


def kernel(
    n_groups, n_ctx, heads, head_size, rows, o_cols,
    hid_hbm, wq_hbm, wo_hbm, gain_hbm, inc_hbm,
    normed_ref, wo_all,
    hid, wq, gain_ref, inc_ref, acc, proj, st_mine, st_peer, st_out, st_in, st_half, st_other,
    load_sem, ring_send, ring_recv, x_send, x_recv, sa_send, sa_recv,
    own_send, own_recv, t_send, t_recv, p_send, p_recv,
):
    n = n_ctx // CORES
    half = n // 2
    snake = 2 if n == 8 else 1
    tokens = hid.shape[0]
    width = heads * head_size
    group = lax.axis_index("groups")
    ctx = lax.axis_index("ctx")
    core = lax.rem(ctx, CORES)
    chip = ctx // CORES
    side = lax.rem(group, 2)
    partner = (group + 1 - 2 * side, ctx)
    peer_ctx = ctx + 1 - 2 * core
    peer = (group, peer_ctx)

    def fold(k):
        if snake == 1:
            return k
        y = lax.rem(k, 2)
        z = k // 2
        return z + y * (n - 1 - 2 * z)

    def unfold(p):
        if snake == 1:
            return p
        y = p // (n // 2)
        z = p + y * (n - 1 - 2 * p)
        return z * 2 + y

    place = fold(chip)

    def chip_at(delta):
        return unfold(lax.rem(place + delta + 2 * n, n))

    to_right = (group, chip_at(1) * CORES + core)
    to_left = (group, chip_at(-1) * CORES + core)

    streams = []

    def cut(kind, unit, pairs):
        base = 0
        for b, a in pairs:
            streams.append((kind, base * unit, b * unit, a * unit))
            base += 2 * b + a

    row_units, col_units = rows // 16, o_cols // 128
    cut(0, 16, shares(row_units, 4))
    cut(1, 16, shares(row_units, 2))
    cut(2, 128, shares(col_units, 2))
    use_x = n_groups % 2 == 0
    if not use_x:
        streams = [(k, base, 0, 2 * b + a) for k, base, b, a in streams]
    count = len(streams)
    hops = [(half, n - 1 - half), (n - 1 - half, half)] * (count // 2)

    def part(kind, dev, start, size):
        if kind < 2:
            at = pl.multiple_of(dev * rows + start, 16)
            return wq.at[pl.ds(at, size), width : 3 * width] if kind == 0 else wq.at[pl.ds(at, size), 0:width]
        return wo_all.at[dev, :, pl.ds(pl.multiple_of(start, 128), size)]

    def ring_part(s, dev):
        kind, base, b, a = streams[s]
        return part(kind, dev, base + side * b, a + b)

    def x_part(s, dev, mine):
        kind, base, b, a = streams[s]
        who = side if mine else 1 - side
        return part(kind, dev, base + who * (a + b), b)

    def whole_part(s, dev):
        kind, base, b, a = streams[s]
        return part(kind, dev, base, a + 2 * b)

    def source(d, h, c):
        return chip_at(-h if d == RIGHT else h) * CORES + c

    def remote(ref, send, recv, target, dst=None):
        return pltpu.make_async_remote_copy(
            src_ref=ref, dst_ref=ref if dst is None else dst, send_sem=send,
            recv_sem=recv, device_id=target, device_id_type=MESH,
        )

    def ring_copy(s, d, h):
        return remote(
            ring_part(s, source(d, h - 1, core)), ring_send.at[s, d, h], ring_recv.at[s, d, h],
            to_right if d == RIGHT else to_left,
        )

    def x_copy(s, d, h, mine=True):
        return remote(x_part(s, source(d, h, core), mine), x_send.at[s, d, h], x_recv.at[s, d, h], partner)

    def sib(s, d, h, c):
        return remote(whole_part(s, source(d, h, c)), sa_send.at[s, d, h], sa_recv.at[s, d, h], peer)

    def sib_own(s, dev):
        return remote(whole_part(s, dev), own_send.at[s], own_recv.at[s], peer)

    loads = [
        pltpu.make_async_copy(wq_hbm, wq.at[pl.ds(pl.multiple_of(ctx * rows, 16), rows), :], load_sem.at[0]),
        pltpu.make_async_copy(wo_hbm, wo_all.at[ctx], load_sem.at[1]),
        pltpu.make_async_copy(hid_hbm, hid, load_sem.at[2]),
        pltpu.make_async_copy(gain_hbm, gain_ref, load_sem.at[3]),
        pltpu.make_async_copy(inc_hbm, inc_ref, load_sem.at[4]),
    ]
    for load in loads:
        load.start()

    barrier = pltpu.get_barrier_semaphore()
    for j in range(1, n):
        other = lax.rem(chip + j, n) * CORES + core
        pl.semaphore_signal(barrier, inc=1, device_id=(group, other), device_id_type=MESH)
    pl.semaphore_signal(barrier, inc=1, device_id=peer, device_id_type=MESH)
    if use_x:
        pl.semaphore_signal(barrier, inc=1, device_id=partner, device_id_type=MESH)
    pl.semaphore_wait(barrier, n + (1 if use_x else 0))

    sent = []

    def go(copy):
        copy.start()
        sent.append(copy)

    def start_stream(s):
        for d in (RIGHT, LEFT):
            if hops[s][d] >= 1:
                go(ring_copy(s, d, 1))
        go(sib_own(s, ctx))

    def arrive(s, d, h):
        ring_copy(s, d, h).wait_recv()
        if h + 1 <= hops[s][d]:
            go(ring_copy(s, d, h + 1))
        if use_x and streams[s][2]:
            go(x_copy(s, d, h))

    def arrive_x(s, d, h):
        if use_x and streams[s][2]:
            x_copy(s, d, h, False).wait_recv()
        go(sib(s, d, h, core))

    def settle(s, d, h):
        sib(s, d, h, 1 - core).wait_recv()

    tile = 256 if tokens % 256 == 0 else tokens

    kv, qq = slice(width, 3 * width), slice(0, width)

    def accumulate(which, columns, first=False):
        at = pl.multiple_of(which * (CORES * rows), 128)
        depth = pl.ds(at, CORES * rows)

        @pl.loop(0, tokens // tile)
        def _(i):
            r = pl.ds(pl.multiple_of(i * tile, tile), tile)
            term = jnp.dot(hid[r, depth], wq[depth, columns], preferred_element_type=jnp.float32)
            if first:
                acc[r, columns] = term
            else:
                acc[r, columns] += term

    def items(which):
        found = []
        for h in range(1, half + 1):
            for s in which:
                for d in (RIGHT, LEFT):
                    if h <= hops[s][d]:
                        found.append((s, d, h))
        return found

    early, late = (0, 1, 2, 3), (4, 5, 6, 7)
    kv_items, late_items = items(early), items(late)
    queue = kv_items + late_items

    def part_key(s, d, h):
        return (streams[s][0], h if d == RIGHT else n - h)

    needed = {}
    for item in queue:
        needed[part_key(*item)] = needed.get(part_key(*item), 0) + 1

    settled = {}

    def settle_and_sum(item):
        settle(*item)
        key = part_key(*item)
        settled[key] = settled.get(key, 0) + 1
        if settled[key] == needed[key] and key[0] < 2:
            accumulate(chip_at(-key[1]), kv if key[0] == 0 else qq)

    position = [0]
    late_start = len(kv_items) - len(early)

    def step():
        i = position[0]
        position[0] = i + 1
        if late_start <= i < late_start + len(late):
            start_stream(late[i - late_start])
        if i < len(queue):
            arrive(*queue[i])
        if 0 <= i - LAG_X < len(queue):
            arrive_x(*queue[i - LAG_X])
        if 0 <= i - LAG_SUM < len(queue):
            settle_and_sum(queue[i - LAG_SUM])

    loads[0].wait()
    start_stream(0)
    start_stream(1)
    loads[1].wait()
    start_stream(2)
    start_stream(3)
    while position[0] < LAG_SUM // 2:
        step()
    for load in loads[2:]:
        load.wait()
    for s in early:
        sib_own(s, peer_ctx).wait_recv()
    accumulate(chip, kv, first=True)
    while position[0] < len(kv_items) + LAG_SUM:
        step()
    proj[:, kv] = acc[:, kv].astype(jnp.bfloat16)

    def cols(kind, h):
        at = kind * width + h * head_size
        return slice(at, at + head_size)

    for h in range(heads):
        st_mine[h] = lax.dot_general(
            proj[:, cols(1, h)], proj[:, cols(2, h)], (((0,), (0,)), ((), ())),
            preferred_element_type=jnp.float32,
        )
    state_copy = remote(st_mine, t_send.at[0], t_recv.at[0], peer, st_peer)
    go(state_copy)

    share = heads // CORES

    def intra(h):
        for i in range(tokens // tile):
            r = slice(i * tile, (i + 1) * tile)
            upto = slice(0, (i + 1) * tile)
            scores = lax.dot_general(
                proj[r, cols(0, h)], proj[upto, cols(1, h)], (((1,), (1,)), ((), ())),
                preferred_element_type=jnp.float32,
            )
            row = lax.broadcasted_iota(jnp.int32, scores.shape, 0) + i * tile
            col = lax.broadcasted_iota(jnp.int32, scores.shape, 1)
            scores = jnp.where(row >= col, scores, 0.0).astype(jnp.bfloat16)
            acc[r, h * head_size : (h + 1) * head_size] = jnp.dot(
                scores, proj[upto, cols(2, h)], preferred_element_type=jnp.float32
            )

    step()
    step()
    state_copy.wait_recv()
    mine = pl.ds(core * share, share)
    st_out[...] = (st_mine[mine] + st_peer[mine]).astype(st_out.dtype)

    def state_to(j):
        target = lax.rem(chip + j, n) * CORES + core
        return remote(st_out, p_send.at[j], p_recv.at[j], (group, target), st_in.at[j])

    for j in range(1, n):
        @pl.when(chip + j < n)
        def _():
            state_to(j).start()

    for s in late:
        sib_own(s, peer_ctx).wait_recv()
    accumulate(chip, qq, first=True)
    while position[0] < len(queue) + LAG_SUM:
        step()

    st_half[...] = jnp.zeros_like(st_half)
    for j in range(1, n):
        @pl.when(chip >= j)
        def _():
            state_to(j).wait_recv()
            st_half[...] += st_in[j].astype(jnp.float32)

    half_copy = remote(st_half, t_send.at[1], t_recv.at[1], peer, st_other)
    go(half_copy)
    proj[:, qq] = acc[:, qq].astype(jnp.bfloat16)
    for h in range(heads):
        intra(h)
    half_copy.wait_recv()

    after = core.astype(jnp.float32)
    for h in range(heads):
        own = (h // share) == core
        low = st_half[h % share]
        high = st_other[h % share]
        prior = inc_ref[h] + jnp.where(own, low, high) + after * st_peer[h]
        top = prior.astype(jnp.bfloat16)
        rest = (prior - top.astype(jnp.float32)).astype(jnp.bfloat16)
        o = slice(h * head_size, (h + 1) * head_size)
        for i in range(tokens // tile):
            r = slice(i * tile, (i + 1) * tile)
            query = proj[r, cols(0, h)]
            mixed = (
                acc[r, o]
                + jnp.dot(query, top, preferred_element_type=jnp.float32)
                + jnp.dot(query, rest, preferred_element_type=jnp.float32)
            )
            scale = lax.rsqrt(jnp.mean(mixed * mixed, axis=-1, keepdims=True) + 1e-06)
            normed_ref[r, o] = (mixed * scale * gain_ref[:, o]).astype(jnp.bfloat16)

    for copy in sent:
        copy.wait_send()
    for j in range(1, n):
        @pl.when(chip + j < n)
        def _():
            state_to(j).wait_send()


def project(x_ref, w_ref, o_ref):
    o_ref[...] = jnp.dot(x_ref[...], w_ref[...], preferred_element_type=jnp.float32).astype(o_ref.dtype)


def local(n_groups, n_ctx, hidden, w_qkv, w_out, norm_gain, incoming):
    tokens, model = hidden.shape
    rows, three = w_qkv.shape
    heads, head_size, _ = incoming.shape
    width = three // 3
    out_rows, out_cols = w_out.shape
    fine = w_out.reshape(16, out_rows * out_cols // 16)
    o_cols = fine.shape[1]
    n = n_ctx // CORES
    half = n // 2
    share = heads // CORES
    dma = pltpu.SemaphoreType.DMA
    state = (heads, head_size, head_size)
    part = (share, head_size, head_size)
    flops = 2 * tokens * model * three
    normed, w_all = pl.pallas_call(
        functools.partial(kernel, n_groups, n_ctx, heads, head_size, rows, o_cols),
        out_shape=(
            jax.ShapeDtypeStruct((tokens, width), jnp.bfloat16),
            jax.ShapeDtypeStruct((n_ctx, 16, o_cols), jnp.bfloat16),
        ),
        in_specs=[pl.BlockSpec(memory_space=pltpu.HBM)] * 5,
        out_specs=(
            pl.BlockSpec(memory_space=pltpu.VMEM),
            pl.BlockSpec(memory_space=pl.ANY),
        ),
        scratch_shapes=[
            pltpu.VMEM((tokens, model), jnp.bfloat16),
            pltpu.VMEM((model, three), jnp.bfloat16),
            pltpu.VMEM((1, width), jnp.float32),
            pltpu.VMEM(state, jnp.float32),
            pltpu.VMEM((tokens, three), jnp.float32),
            pltpu.VMEM((tokens, three), jnp.bfloat16),
            pltpu.VMEM(state, jnp.float32),
            pltpu.VMEM(state, jnp.float32),
            pltpu.VMEM(part, jnp.bfloat16),
            pltpu.VMEM((n,) + part, jnp.bfloat16),
            pltpu.VMEM(part, jnp.float32),
            pltpu.VMEM(part, jnp.float32),
            dma((5,)),
        ]
        + [dma((8, 2, half + 1))] * 6
        + [dma((8,)), dma((8,)), dma((2,)), dma((2,)), dma((n,)), dma((n,))],
        compiler_params=pltpu.CompilerParams(
            collective_id=0, has_side_effects=True, vmem_limit_bytes=48 * 1024 * 1024
        ),
        cost_estimate=pl.CostEstimate(
            flops=flops, bytes_accessed=tokens * model * 2, transcendentals=0
        ),
    )(hidden, w_qkv, fine, norm_gain.reshape(1, width), incoming)
    w_full = w_all.reshape(n_ctx * out_rows, out_cols)
    block = 256 if tokens % 256 == 0 else tokens
    return pl.pallas_call(
        project,
        grid=(tokens // block,),
        out_shape=jax.ShapeDtypeStruct((tokens, out_cols), jnp.bfloat16),
        in_specs=[
            pl.BlockSpec((block, width), lambda i: (i, 0)),
            pl.BlockSpec((width, out_cols), lambda i: (0, 0)),
        ],
        out_specs=pl.BlockSpec((block, out_cols), lambda i: (i, 0)),
        compiler_params=pltpu.CompilerParams(vmem_limit_bytes=32 * 1024 * 1024),
        cost_estimate=pl.CostEstimate(
            flops=2 * tokens * width * out_cols, bytes_accessed=2 * tokens * out_cols, transcendentals=0
        ),
    )(normed, w_full)


def solution(mesh):
    body = functools.partial(local, mesh.shape["groups"], mesh.shape["ctx"])
    return jax.shard_map(
        body,
        mesh=mesh,
        in_specs=(
            P(("groups", "ctx"), None),
            P("ctx", None),
            P("ctx", None),
            P(),
            P("groups", None, None),
        ),
        out_specs=P(("groups", "ctx"), None),
        check_vma=False,
    )
```
